32 devices in a mesh: out: 16 (over z, x, core), in: 2 (over y).
Axes of the slice: x: 2, y: 2, z: 4, core: 2. Of those that a mesh axis runs over, the one named last changes fastest.
Arguments:
- slopes: bfloat16 [128, 163840], P('out', 'in'), may hold values from -6 to 6
- cols_first: int32 [128, 16], P(None, 'in'), may hold values from 0 to 319
- count_first: int32 [128, 2], P('out', 'in'), may hold values from 1 to 8
- weight_first: bfloat16 [128, 16, 256, 256], P('out', 'in'), may hold values from -0.125 to 0.125
- bias_first: float32 [32768], P(('out', 'in')), may hold values from -3 to 3
- cols_second: int32 [128, 8], P('out', 'in'), may hold values from 0 to 63
- count_second: int32 [128, 2], P('out', 'in'), may hold values from 1 to 4
- weight_second: bfloat16 [128, 8, 256, 256], P('out', 'in'), may hold values from -0.1875 to 0.1875
- bias_second: float32 [32768], P(('out', 'in')), may hold values from -3 to 3
- cotangent: bfloat16 [128, 32768], P(None, ('out', 'in')), may hold values from -6 to 6
Outputs:
- estimate: bfloat16 [128, 32768], P(None, ('out', 'in'))
- grad_first: bfloat16 [128, 16, 256, 256], P('out', 'in')
- grad_second: bfloat16 [128, 8, 256, 256], P('out', 'in')
The draws below stay inside these ranges and needn't reach their ends.
Inputs may be any that keep to these rules, and one draw needn't show every extreme that they name: `cols_first`: A local block index within the range of slopes of the slot's in index. `count_first`: slots of a block row at or after this count, within one in range, are not used. `cols_second`: A local block index within the range of reordered hidden units of the slot's in index. `count_second`: slots of a block row at or after this count, within one in range, are not used.
All inputs are finite; a program needn't handle non-finite values.
Results may differ from the reference program's by a relative error of at most 0.025.
Values may be sent and summed in bfloat16 or wider, within the bound.
A program may use at most 128 MiB of HBM per device.

```python
import jax
import jax.numpy as jnp
from jax import lax

SLOPES = 163840
HIDDEN_SIZE = 32768
BLK = 256
KD1 = 8
KD2 = 4
FRAMES = 128
HB = 128
CB1 = 320
CB2 = 64
SUB = 1024
N_OUT = 16
N_IN = 2


def plant(drawn, key, least, top_value):
    longest = drawn.shape.index(max(drawn.shape))
    spots = []
    for shift in (0, 1):
        where = [jax.random.randint(jax.random.fold_in(key, axis), (), 0, length) for axis, length in enumerate(drawn.shape)]
        where[longest] = (where[longest] + shift) % drawn.shape[longest]
        spots.append(tuple(where))
    return drawn.at[spots[0]].set(least).at[spots[1]].set(top_value)


def shard_levels(own_key, extent, pieces, smallest, top_value):
    gain, own = 1.0, jax.random.fold_in(own_key, 6)
    for dim, blocks in pieces:
        draws = jnp.exp(jax.random.uniform(jax.random.fold_in(own, dim), (blocks,), jnp.float32, smallest / len(pieces), top_value / len(pieces)))
        gain = gain * jnp.repeat(draws, extent[dim] // blocks).reshape([-1 if axis == dim else 1 for axis in range(len(extent))])
    return gain


def centred(own_key, extent, scale, most, pieces=(), kind=jnp.bfloat16):
    drawn = scale * jax.random.normal(own_key, extent, jnp.float32)
    if pieces:
        drawn = drawn * shard_levels(own_key, extent, pieces, -0.22, 0.18)
    return jnp.clip(drawn, -most, most).astype(kind)


def setup_inputs(seed: int = 0) -> dict:
    splits = jax.random.split(jax.random.key(seed), 11)
    return {
        "slopes": centred(splits[0], (FRAMES, SLOPES), 1.0, 6.0, ((0, 16), (1, 2))),
        "cols_first": plant(jax.random.randint(splits[1], (HB, N_IN * KD1), 0, CB1), jax.random.fold_in(splits[1], 1), 0, CB1 - 1).astype(jnp.int32),
        "count_first": plant(jax.random.randint(splits[2], (HB, N_IN), 1, KD1 + 1), jax.random.fold_in(splits[2], 1), 1, KD1).astype(jnp.int32),
        "weight_first": centred(splits[3], (HB, N_IN * KD1, BLK, BLK), (BLK * N_IN * KD1 // 2) ** -0.5, 0.125, ((0, 16), (1, 2))),
        "bias_first": centred(splits[4], (HIDDEN_SIZE,), 0.5, 3.0, ((0, 32),), jnp.float32),
        "cols_second": plant(jax.random.randint(splits[5], (HB, N_IN * KD2), 0, CB2), jax.random.fold_in(splits[5], 1), 0, CB2 - 1).astype(jnp.int32),
        "count_second": plant(jax.random.randint(splits[6], (HB, N_IN), 1, KD2 + 1), jax.random.fold_in(splits[6], 1), 1, KD2).astype(jnp.int32),
        "weight_second": centred(splits[7], (HB, N_IN * KD2, BLK, BLK), (BLK * N_IN * KD2 // 2) ** -0.5, 0.1875, ((0, 16), (1, 2))),
        "bias_second": centred(splits[8], (HIDDEN_SIZE,), 0.5, 3.0, ((0, 32),), jnp.float32),
        "cotangent": centred(splits[9], (FRAMES, HIDDEN_SIZE), 1.0, 6.0, ((1, 32),)),
    }


def live_mask(counts, slots):
    column = jnp.arange(counts.shape[1] * slots, dtype=jnp.int32)
    spread = jnp.repeat(counts, slots, axis=1)
    return (column[None, :] % slots < spread).astype(jnp.float32)

def block_index(cols, blocks, slots):
    column = jnp.arange(cols.shape[1], dtype=jnp.int32)
    return ((column // slots)[None, :] * blocks + cols).astype(jnp.int32)

def to_second(values):
    return values.reshape(FRAMES, N_OUT, N_IN, SUB).transpose(0, 2, 1, 3).reshape(FRAMES, HIDDEN_SIZE)

def from_second(values):
    return values.reshape(FRAMES, N_IN, N_OUT, SUB).transpose(0, 2, 1, 3).reshape(FRAMES, HIDDEN_SIZE)

def layer_forward(inputs, index, weights, live, bias):
    blocks = inputs.reshape(FRAMES, -1, BLK)

    def one_row(operands):
        row_index, row_weight, row_live = operands
        taken = jnp.take(blocks, row_index, axis=1).astype(jnp.float32)
        masked = row_weight.astype(jnp.float32) * row_live[:, None, None]
        return jnp.einsum('fkb,kbo->fo', taken, masked)
    rows = lax.map(one_row, (index, weights, live))
    return jnp.transpose(rows, (1, 0, 2)).reshape(FRAMES, HIDDEN_SIZE) + bias[None, :]

def layer_weight_grad(inputs, index, live, delta):
    blocks = inputs.reshape(FRAMES, -1, BLK)
    delta_rows = jnp.transpose(delta.reshape(FRAMES, HB, BLK), (1, 0, 2))

    def one_row(operands):
        row_index, row_live, row_delta = operands
        taken = jnp.take(blocks, row_index, axis=1).astype(jnp.float32)
        grad = jnp.einsum('fkb,fo->kbo', taken, row_delta.astype(jnp.float32))
        return (grad * row_live[:, None, None]).astype(jnp.bfloat16)
    return lax.map(one_row, (index, live, delta_rows))

def layer_adjoint(index, weights, live, delta, width):
    delta_rows = jnp.transpose(delta.reshape(FRAMES, HB, BLK), (1, 0, 2))

    def one_row(total, operands):
        row_index, row_weight, row_live, row_delta = operands
        masked = row_weight.astype(jnp.float32) * row_live[:, None, None]
        term = jnp.einsum('fo,kbo->fkb', row_delta.astype(jnp.float32), masked)
        return (total.at[:, row_index, :].add(term), None)
    start = jnp.zeros((FRAMES, width // BLK, BLK), jnp.float32)
    total, unused = lax.scan(one_row, start, (index, weights, live, delta_rows))
    return total.reshape(FRAMES, width)

def reference(slopes, cols_first, count_first, weight_first, bias_first, cols_second, count_second, weight_second, bias_second, cotangent):
    live_first = live_mask(count_first, KD1)
    live_second = live_mask(count_second, KD2)
    index_first = block_index(cols_first, CB1, KD1)
    index_second = block_index(cols_second, CB2, KD2)
    hidden_first = jnp.tanh(layer_forward(slopes, index_first, weight_first, live_first, bias_first)).astype(jnp.bfloat16)
    ordered = to_second(hidden_first)
    estimate = jnp.tanh(layer_forward(ordered, index_second, weight_second, live_second, bias_second)).astype(jnp.bfloat16)
    est32 = estimate.astype(jnp.float32)
    delta_second = (cotangent.astype(jnp.float32) * (1.0 - est32 * est32)).astype(jnp.bfloat16)
    grad_second = layer_weight_grad(ordered, index_second, live_second, delta_second)
    back_ordered = layer_adjoint(index_second, weight_second, live_second, delta_second, HIDDEN_SIZE)
    back_first = from_second(back_ordered)
    hid32 = hidden_first.astype(jnp.float32)
    delta_first = (back_first * (1.0 - hid32 * hid32)).astype(jnp.bfloat16)
    grad_first = layer_weight_grad(slopes, index_first, live_first, delta_first)
    return (estimate, grad_first, grad_second)
```

```python
import functools

import jax
import jax.numpy as jnp
from jax import lax
from jax.experimental import pallas as pl
from jax.experimental.pallas import tpu as pltpu
from jax.sharding import PartitionSpec as P

BLK = 256
KD1 = 8
KD2 = 4
VMEM_LIMIT = 48 * 1024 * 1024
F32 = jnp.float32
BF16 = jnp.bfloat16


def params():
    return pltpu.CompilerParams(vmem_limit_bytes=VMEM_LIMIT)


def panel_block(frames, sub):
    return (1, frames, BLK) if sub >= BLK else (BLK // sub, frames, sub)


def panel_place(sub, block):
    if sub >= BLK:
        per = sub // BLK
        return (block // per, 0, block % per)
    return (block, 0, 0)


def read_panel(ref):
    if len(ref.shape) == 2:
        return ref[...]
    parts = [ref[i] for i in range(ref.shape[0])]
    return parts[0] if len(parts) == 1 else jnp.concatenate(parts, axis=1)


def write_panel(ref, value):
    width = ref.shape[2]
    for i in range(ref.shape[0]):
        ref[i] = value[:, i * width : (i + 1) * width].astype(ref.dtype)


def forward_kernel(slots, cols, counts, *refs):
    panels, weight, out = refs[:slots], refs[slots], refs[slots + 1]
    live = counts[pl.program_id(0)]
    total = None
    for k in range(slots):
        term = jnp.dot(read_panel(panels[k]), weight[0, k], preferred_element_type=F32)
        term = jnp.where(k < live, term, 0.0)
        total = term if total is None else total + term
    write_panel(out, total)


def grad_kernel(slots, cols, counts, *refs):
    panels, delta, out = refs[:slots], refs[slots], refs[slots + 1]
    live = counts[pl.program_id(0)]
    rows = read_panel(delta)
    for k in range(slots):
        term = lax.dot_general(
            read_panel(panels[k]), rows, (((0,), (0,)), ((), ())), preferred_element_type=F32
        )
        out[0, k] = jnp.where(k < live, term, 0.0).astype(out.dtype)


def adjoint_kernel(slots, cols, counts, delta, weight, out, total):
    row = pl.program_id(0)
    live = counts[row]

    @pl.when(row == 0)
    def _():
        total[...] = jnp.zeros_like(total)

    rows = read_panel(delta)
    for k in range(slots):
        term = lax.dot_general(
            rows, weight[0, k], (((1,), (1,)), ((), ())), preferred_element_type=F32
        )
        place = cols[row * slots + k]
        total[place] += jnp.where(k < live, term, 0.0)

    @pl.when(row == pl.num_programs(0) - 1)
    def _():
        pieces, frames, sub = out.shape
        if sub >= BLK:
            per = sub // BLK
            for c in range(total.shape[0]):
                at = (c % per) * BLK
                out[c // per, :, at : at + BLK] = total[c].astype(out.dtype)
        else:
            per = BLK // sub
            for p in range(pieces):
                at = (p % per) * sub
                out[p] = total[p // per, :, at : at + sub].astype(out.dtype)


def panel_specs(slots, frames, sub):
    def spec(k):
        if sub is None:
            return pl.BlockSpec((frames, BLK), lambda r, cols, counts: (0, cols[r * slots + k]))
        return pl.BlockSpec(
            panel_block(frames, sub),
            lambda r, cols, counts: panel_place(sub, cols[r * slots + k]),
        )

    return [spec(k) for k in range(slots)]


def row_spec(frames, sub):
    return pl.BlockSpec(panel_block(frames, sub), lambda r, cols, counts: panel_place(sub, r))


def weight_spec(slots):
    return pl.BlockSpec((1, slots, BLK, BLK), lambda r, cols, counts: (r, 0, 0, 0))


def forward(inputs, in_sub, cols, counts, weight, frames, pieces, sub):
    rows, slots = weight.shape[:2]
    return pl.pallas_call(
        functools.partial(forward_kernel, slots),
        grid_spec=pltpu.PrefetchScalarGridSpec(
            num_scalar_prefetch=2,
            grid=(rows,),
            in_specs=panel_specs(slots, frames, in_sub) + [weight_spec(slots)],
            out_specs=row_spec(frames, sub),
        ),
        out_shape=jax.ShapeDtypeStruct((pieces, frames, sub), F32),
        compiler_params=params(),
    )(cols, counts, *([inputs] * slots), weight)


def weight_grad(inputs, in_sub, cols, counts, delta, slots):
    pieces, frames, sub = delta.shape
    rows = pieces * sub // BLK
    return pl.pallas_call(
        functools.partial(grad_kernel, slots),
        grid_spec=pltpu.PrefetchScalarGridSpec(
            num_scalar_prefetch=2,
            grid=(rows,),
            in_specs=panel_specs(slots, frames, in_sub) + [row_spec(frames, sub)],
            out_specs=weight_spec(slots),
        ),
        out_shape=jax.ShapeDtypeStruct((rows, slots, BLK, BLK), BF16),
        cost_estimate=pl.CostEstimate(
            flops=2 * rows * slots * frames * BLK * BLK,
            bytes_accessed=2 * rows * slots * BLK * (BLK + frames),
            transcendentals=0,
        ),
        compiler_params=params(),
    )(cols, counts, *([inputs] * slots), delta)


def adjoint(delta, weight, cols, counts, out_pieces):
    pieces, frames, sub = delta.shape
    rows, slots = weight.shape[:2]
    return pl.pallas_call(
        functools.partial(adjoint_kernel, slots),
        grid_spec=pltpu.PrefetchScalarGridSpec(
            num_scalar_prefetch=2,
            grid=(rows,),
            in_specs=[row_spec(frames, sub), weight_spec(slots)],
            out_specs=pl.BlockSpec((out_pieces, frames, sub), lambda r, cols, counts: (0, 0, 0)),
            scratch_shapes=[pltpu.VMEM((out_pieces * sub // BLK, frames, BLK), F32)],
        ),
        out_shape=jax.ShapeDtypeStruct((out_pieces, frames, sub), BF16),
        compiler_params=params(),
    )(cols, counts, delta, weight)


def shards(
    n_out,
    n_in,
    slopes,
    cols_first,
    count_first,
    weight_first,
    bias_first,
    cols_second,
    count_second,
    weight_second,
    bias_second,
    cotangent,
):
    rows = weight_first.shape[0]
    frames = slopes.shape[0] * n_out
    sub = bias_first.shape[0]
    first = lax.dynamic_slice_in_dim(cols_first, lax.axis_index("out") * rows, rows, 0).reshape(-1)
    second = cols_second.reshape(-1)
    live_first, live_second = count_first.reshape(-1), count_second.reshape(-1)

    gathered = lax.all_gather(slopes, "out", axis=0, tiled=True)
    partial_first = forward(gathered, None, first, live_first, weight_first, frames, n_in, sub)
    summed_first = lax.psum_scatter(partial_first, "in", scatter_dimension=0, tiled=False)
    hidden = jnp.tanh(summed_first + bias_first[None, :]).astype(BF16)

    ordered = lax.all_gather(hidden, "out", axis=0, tiled=False)
    partial_second = forward(ordered, sub, second, live_second, weight_second, frames, n_in, sub)
    summed_second = lax.psum_scatter(partial_second, "in", scatter_dimension=0, tiled=False)
    estimate = jnp.tanh(summed_second + bias_second[None, :]).astype(BF16)
    est32 = estimate.astype(F32)
    delta_second = (cotangent.astype(F32) * (1.0 - est32 * est32)).astype(BF16)

    rows_second = lax.all_gather(delta_second, "in", axis=0, tiled=False)
    spread = adjoint(rows_second, weight_second, second, live_second, n_out)
    back = lax.psum_scatter(spread, "out", scatter_dimension=0, tiled=False).astype(F32)
    grad_second = weight_grad(ordered, sub, second, live_second, rows_second, KD2)
    hid32 = hidden.astype(F32)
    delta_first = (back * (1.0 - hid32 * hid32)).astype(BF16)
    rows_first = lax.all_gather(delta_first, "in", axis=0, tiled=False)
    grad_first = weight_grad(gathered, None, first, live_first, rows_first, KD1)
    return (estimate, grad_first, grad_second)


def solution(mesh):
    return jax.shard_map(
        functools.partial(shards, mesh.shape["out"], mesh.shape["in"]),
        mesh=mesh,
        in_specs=(
            P("out", "in"),
            P(None, "in"),
            P("out", "in"),
            P("out", "in", None, None),
            P(("out", "in")),
            P("out", "in"),
            P("out", "in"),
            P("out", "in", None, None),
            P(("out", "in")),
            P(None, ("out", "in")),
        ),
        out_specs=(P(None, ("out", "in")), P("out", "in", None, None), P("out", "in", None, None)),
        check_vma=False,
    )
```

```python
import functools

import jax
import jax.numpy as jnp
from jax import lax
from jax.experimental import pallas as pl
from jax.experimental.pallas import tpu as pltpu
from jax.sharding import PartitionSpec as P

BLK = 256
KD1 = 8
KD2 = 4
VMEM_LIMIT = 48 * 1024 * 1024
F32 = jnp.float32
BF16 = jnp.bfloat16


def params():
    return pltpu.CompilerParams(vmem_limit_bytes=VMEM_LIMIT)


def panel_block(frames, sub):
    return (1, frames, BLK) if sub >= BLK else (BLK // sub, frames, sub)


def panel_place(sub, block):
    if sub >= BLK:
        per = sub // BLK
        return (block // per, 0, block % per)
    return (block, 0, 0)


def read_panel(ref):
    if len(ref.shape) == 2:
        return ref[...]
    parts = [ref[i] for i in range(ref.shape[0])]
    return parts[0] if len(parts) == 1 else jnp.concatenate(parts, axis=1)


def write_panel(ref, value):
    width = ref.shape[2]
    for i in range(ref.shape[0]):
        ref[i] = value[:, i * width : (i + 1) * width].astype(ref.dtype)


def forward_kernel(slots, cols, counts, *refs):
    panels, weight, out = refs[:slots], refs[slots], refs[slots + 1]
    live = counts[pl.program_id(0)]
    total = None
    for k in range(slots):
        term = jnp.dot(read_panel(panels[k]), weight[0, k], preferred_element_type=F32)
        term = jnp.where(k < live, term, 0.0)
        total = term if total is None else total + term
    write_panel(out, total)


def grad_kernel(slots, cols, counts, *refs):
    panels, delta, out = refs[:slots], refs[slots], refs[slots + 1]
    live = counts[pl.program_id(0)]
    rows = read_panel(delta)
    for k in range(slots):
        term = lax.dot_general(
            read_panel(panels[k]), rows, (((0,), (0,)), ((), ())), preferred_element_type=F32
        )
        out[0, k] = jnp.where(k < live, term, 0.0).astype(out.dtype)


def adjoint_kernel(slots, cols, counts, delta, weight, out, total):
    row = pl.program_id(0)
    live = counts[row]

    @pl.when(row == 0)
    def _():
        total[...] = jnp.zeros_like(total)

    rows = read_panel(delta)
    for k in range(slots):
        term = lax.dot_general(
            rows, weight[0, k], (((1,), (1,)), ((), ())), preferred_element_type=F32
        )
        place = cols[row * slots + k]
        total[place] += jnp.where(k < live, term, 0.0)

    @pl.when(row == pl.num_programs(0) - 1)
    def _():
        pieces, frames, sub = out.shape
        if sub >= BLK:
            per = sub // BLK
            for c in range(total.shape[0]):
                at = (c % per) * BLK
                out[c // per, :, at : at + BLK] = total[c].astype(out.dtype)
        else:
            per = BLK // sub
            for p in range(pieces):
                at = (p % per) * sub
                out[p] = total[p // per, :, at : at + sub].astype(out.dtype)


def panel_specs(slots, frames, sub):
    def spec(k):
        if sub is None:
            return pl.BlockSpec((frames, BLK), lambda r, cols, counts: (0, cols[r * slots + k]))
        return pl.BlockSpec(
            panel_block(frames, sub),
            lambda r, cols, counts: panel_place(sub, cols[r * slots + k]),
        )

    return [spec(k) for k in range(slots)]


def row_spec(frames, sub):
    return pl.BlockSpec(panel_block(frames, sub), lambda r, cols, counts: panel_place(sub, r))


def weight_spec(slots):
    return pl.BlockSpec((1, slots, BLK, BLK), lambda r, cols, counts: (r, 0, 0, 0))


def forward(inputs, in_sub, cols, counts, weight, frames, pieces, sub):
    rows, slots = weight.shape[:2]
    return pl.pallas_call(
        functools.partial(forward_kernel, slots),
        grid_spec=pltpu.PrefetchScalarGridSpec(
            num_scalar_prefetch=2,
            grid=(rows,),
            in_specs=panel_specs(slots, frames, in_sub) + [weight_spec(slots)],
            out_specs=row_spec(frames, sub),
        ),
        out_shape=jax.ShapeDtypeStruct((pieces, frames, sub), F32),
        compiler_params=params(),
    )(cols, counts, *([inputs] * slots), weight)


def weight_grad(inputs, in_sub, cols, counts, delta, slots):
    pieces, frames, sub = delta.shape
    rows = pieces * sub // BLK
    return pl.pallas_call(
        functools.partial(grad_kernel, slots),
        grid_spec=pltpu.PrefetchScalarGridSpec(
            num_scalar_prefetch=2,
            grid=(rows,),
            in_specs=panel_specs(slots, frames, in_sub) + [row_spec(frames, sub)],
            out_specs=weight_spec(slots),
        ),
        out_shape=jax.ShapeDtypeStruct((rows, slots, BLK, BLK), BF16),
        cost_estimate=pl.CostEstimate(
            flops=2 * rows * slots * frames * BLK * BLK,
            bytes_accessed=2 * rows * slots * BLK * (BLK + frames),
            transcendentals=0,
        ),
        compiler_params=params(),
    )(cols, counts, *([inputs] * slots), delta)


def adjoint(delta, weight, cols, counts, out_pieces):
    pieces, frames, sub = delta.shape
    rows, slots = weight.shape[:2]
    return pl.pallas_call(
        functools.partial(adjoint_kernel, slots),
        grid_spec=pltpu.PrefetchScalarGridSpec(
            num_scalar_prefetch=2,
            grid=(rows,),
            in_specs=[row_spec(frames, sub), weight_spec(slots)],
            out_specs=pl.BlockSpec((out_pieces, frames, sub), lambda r, cols, counts: (0, 0, 0)),
            scratch_shapes=[pltpu.VMEM((out_pieces * sub // BLK, frames, BLK), F32)],
        ),
        out_shape=jax.ShapeDtypeStruct((out_pieces, frames, sub), BF16),
        compiler_params=params(),
    )(cols, counts, delta, weight)


MESH = pl.DeviceIdType.MESH
STEP = 16
SIDE = 4


def by_rows(frames, body):
    def turn(i, carry):
        body(pl.ds(pl.multiple_of(i * STEP, STEP), STEP))
        return carry

    lax.fori_loop(0, frames // STEP, turn, 0)


def remote(source, target, send, recv, peer):
    return pltpu.make_async_remote_copy(
        src_ref=source,
        dst_ref=target,
        send_sem=send,
        recv_sem=recv,
        device_id=peer,
        device_id_type=MESH,
    )


def greet(peers):
    barrier = pltpu.get_barrier_semaphore()
    for peer in peers:
        pl.semaphore_signal(barrier, inc=1, device_id=peer, device_id_type=MESH)
    pl.semaphore_wait(barrier, len(peers))


def in_peers(n_in):
    me = lax.axis_index("in")
    return [{"in": lax.rem(me + t, n_in)} for t in range(1, n_in)]


def out_place(n_out):
    me = lax.axis_index("out")
    inner = lax.rem(me, SIDE)
    core = lax.rem(me, 2)
    column = lax.rem(lax.div(me, 2), 2)
    return me, lax.div(me, SIDE), inner, me + 1 - 2 * core, me + 2 - 4 * column


def out_peers(n_out):
    me, outer, inner, core_peer, x_peer = out_place(n_out)
    count = n_out // SIDE
    far = [{"out": lax.rem(outer + t, count) * SIDE + inner} for t in range(1, count)]
    return [{"out": core_peer}, {"out": x_peer}] + far


def exchange_start(n_in, partial, leaving, arriving, send, recv):
    copies = []
    for t, peer in enumerate(in_peers(n_in)):
        def cast(at, t=t, peer=peer):
            leaving[t, at, :] = partial[peer["in"], at, :].astype(BF16)

        by_rows(partial.shape[1], cast)
        copy = remote(leaving.at[t], arriving.at[t], send.at[t], recv.at[t], peer)
        copy.start()
        copies.append(copy)
    for copy in copies:
        copy.wait()


def exchanged(n_in, partial, arriving, bias, at):
    total = partial[lax.axis_index("in"), at, :]
    for t in range(n_in - 1):
        total = total + arriving[t, at, :].astype(F32)
    return total + bias[...]


def share_in(n_in, rows, send, recv):
    me = lax.axis_index("in")
    copies = []
    for t, peer in enumerate(in_peers(n_in)):
        copy = remote(rows.at[me], rows.at[me], send.at[t], recv.at[t], peer)
        copy.start()
        copies.append(copy)
    for copy in copies:
        copy.wait()


def hidden_kernel(
    n_out, n_in, partial, bias, hidden, ordered, leaving, arriving, in_send, in_recv, send, recv, own
):
    frames = hidden.shape[0]
    greet(in_peers(n_in) + out_peers(n_out))
    exchange_start(n_in, partial, leaving, arriving, in_send, in_recv)

    def finish(at):
        hidden[at, :] = jnp.tanh(exchanged(n_in, partial, arriving, bias, at)).astype(BF16)

    by_rows(frames, finish)
    me, outer, inner, core_peer, x_peer = out_place(n_out)
    count = n_out // SIDE
    copies = []

    def forward_to(source, block, target):
        k = len(copies)
        copy = remote(source, ordered.at[block], send.at[k], recv.at[block], {"out": target})
        copy.start()
        copies.append(copy)

    def arrived(block):
        remote(hidden, ordered.at[block], send.at[0], recv.at[block], {"out": core_peer}).wait_recv()

    def held(t, place):
        return lax.rem(outer + t, count) * SIDE + place

    for t in range(1, count):
        forward_to(hidden, me, held(t, inner))
    forward_to(hidden, me, x_peer)
    forward_to(hidden, me, core_peer)
    keep = pltpu.make_async_copy(hidden, ordered.at[me], own)
    keep.start()
    across = lax.rem(x_peer, SIDE)
    for t in range(1, count + 1):
        if t < count:
            block = held(t, inner)
            arrived(block)
            forward_to(ordered.at[block], block, x_peer)
            forward_to(ordered.at[block], block, core_peer)
        block = held(t - 1, across)
        arrived(block)
        forward_to(ordered.at[block], block, core_peer)
    for t in range(count):
        for place in (lax.rem(core_peer, SIDE), SIDE - 1 - inner):
            arrived(held(t, place))
    for copy in copies:
        copy.wait_send()
    keep.wait()


def estimate_kernel(
    n_in, partial, bias, cotangent, estimate, rows, leaving, arriving, in_send, in_recv, send, recv
):
    greet(in_peers(n_in))
    exchange_start(n_in, partial, leaving, arriving, in_send, in_recv)
    me = lax.axis_index("in")

    def finish(at):
        value = jnp.tanh(exchanged(n_in, partial, arriving, bias, at)).astype(BF16)
        estimate[at, :] = value
        wide = value.astype(F32)
        rows[me, at, :] = (cotangent[at, :].astype(F32) * (1.0 - wide * wide)).astype(BF16)

    by_rows(estimate.shape[0], finish)
    share_in(n_in, rows, send, recv)


def reduce_kernel(
    n_out, n_in, spread, hidden, rows,
    from_core, to_x, from_x, to_z, from_z,
    core_send, core_recv, x_send, x_recv, z_send, z_recv, in_send, in_recv,
):
    frames = hidden.shape[0]
    count = n_out // SIDE
    greet(in_peers(n_in) + out_peers(n_out))
    me, outer, inner, core_peer, x_peer = out_place(n_out)
    across = lax.rem(x_peer, SIDE)
    core_inner, core_across = lax.rem(core_peer, SIDE), SIDE - 1 - inner

    def held(t, place):
        return lax.rem(outer + t, count) * SIDE + place

    core_copies, x_copies, z_copies = [], [], []
    for t in range(1, count + 1):
        for place in (core_across, core_inner):
            k = len(core_copies)
            copy = remote(
                spread.at[held(t, place)], from_core.at[k], core_send.at[k], core_recv.at[k],
                {"out": core_peer},
            )
            copy.start()
            core_copies.append(copy)

    def column_sum(t, at):
        total = spread[held(t, inner), at, :].astype(F32)
        total = total + from_core[2 * t - 1, at, :].astype(F32)
        return total + from_x[t - 1, at, :].astype(F32)

    for t in range(1, count + 2):
        if t <= count:
            core_copies[2 * t - 2].wait_recv()

            def add_core(at, t=t):
                total = spread[held(t, across), at, :].astype(F32)
                to_x[t - 1, at, :] = (total + from_core[2 * t - 2, at, :].astype(F32)).astype(BF16)

            by_rows(frames, add_core)
            copy = remote(
                to_x.at[t - 1], from_x.at[t - 1], x_send.at[t - 1], x_recv.at[t - 1],
                {"out": x_peer},
            )
            copy.start()
            x_copies.append(copy)
        s = t - 1
        if s >= 1:
            core_copies[2 * s - 1].wait_recv()
            x_copies[s - 1].wait_recv()
        if 1 <= s < count:

            def add_x(at, s=s):
                to_z[s - 1, at, :] = column_sum(s, at).astype(BF16)

            by_rows(frames, add_x)
            copy = remote(
                to_z.at[s - 1], from_z.at[s - 1], z_send.at[s - 1], z_recv.at[s - 1],
                {"out": held(s, inner)},
            )
            copy.start()
            z_copies.append(copy)
    for copy in z_copies:
        copy.wait_recv()
    place = lax.axis_index("in")

    def finish(at):
        total = column_sum(count, at)
        for s in range(count - 1):
            total = total + from_z[s, at, :].astype(F32)
        wide = hidden[at, :].astype(F32)
        rows[place, at, :] = (total * (1.0 - wide * wide)).astype(BF16)

    by_rows(frames, finish)
    share_in(n_in, rows, in_send, in_recv)
    for copy in core_copies + x_copies + z_copies:
        copy.wait_send()


def whole_specs(count):
    return [pl.BlockSpec(memory_space=pltpu.VMEM)] * count


def dma(count):
    return pltpu.SemaphoreType.DMA((count,))


def remote_params(collective_id):
    return pltpu.CompilerParams(
        collective_id=collective_id, has_side_effects=True, vmem_limit_bytes=VMEM_LIMIT
    )


def hidden_layer(n_out, n_in, partial, bias):
    _, frames, sub = partial.shape
    return pl.pallas_call(
        functools.partial(hidden_kernel, n_out, n_in),
        out_shape=(
            jax.ShapeDtypeStruct((frames, sub), BF16),
            jax.ShapeDtypeStruct((n_out, frames, sub), BF16),
        ),
        in_specs=whole_specs(2),
        out_specs=(pl.BlockSpec(memory_space=pltpu.VMEM), pl.BlockSpec(memory_space=pl.ANY)),
        scratch_shapes=[
            pltpu.VMEM((n_in - 1, frames, sub), BF16),
            pltpu.VMEM((n_in - 1, frames, sub), BF16),
            dma(n_in - 1),
            dma(n_in - 1),
            dma(n_out),
            dma(n_out),
            pltpu.SemaphoreType.DMA,
        ],
        compiler_params=remote_params(1),
    )(partial, bias.reshape(1, -1))


def estimate_layer(n_in, partial, bias, cotangent):
    _, frames, sub = partial.shape
    return pl.pallas_call(
        functools.partial(estimate_kernel, n_in),
        out_shape=(
            jax.ShapeDtypeStruct((frames, sub), BF16),
            jax.ShapeDtypeStruct((n_in, frames, sub), BF16),
        ),
        in_specs=whole_specs(3),
        out_specs=tuple(whole_specs(2)),
        scratch_shapes=[
            pltpu.VMEM((n_in - 1, frames, sub), BF16),
            pltpu.VMEM((n_in - 1, frames, sub), BF16),
            dma(n_in - 1),
            dma(n_in - 1),
            dma(n_in - 1),
            dma(n_in - 1),
        ],
        compiler_params=remote_params(2),
    )(partial, bias.reshape(1, -1), cotangent)


def reduce_layer(n_out, n_in, spread, hidden):
    _, frames, sub = spread.shape
    count = n_out // SIDE
    blocks = lambda n: pltpu.VMEM((n, frames, sub), BF16)
    return pl.pallas_call(
        functools.partial(reduce_kernel, n_out, n_in),
        out_shape=jax.ShapeDtypeStruct((n_in, frames, sub), BF16),
        in_specs=whole_specs(2),
        out_specs=pl.BlockSpec(memory_space=pltpu.VMEM),
        scratch_shapes=[
            blocks(2 * count), blocks(count), blocks(count), blocks(count - 1), blocks(count - 1),
            dma(2 * count), dma(2 * count), dma(count), dma(count), dma(count - 1), dma(count - 1),
            dma(n_in - 1), dma(n_in - 1),
        ],
        compiler_params=remote_params(3),
    )(spread, hidden)


def shards(
    n_out,
    n_in,
    slopes,
    cols_first,
    count_first,
    weight_first,
    bias_first,
    cols_second,
    count_second,
    weight_second,
    bias_second,
    cotangent,
):
    rows = weight_first.shape[0]
    frames = slopes.shape[0] * n_out
    sub = bias_first.shape[0]
    first = lax.dynamic_slice_in_dim(cols_first, lax.axis_index("out") * rows, rows, 0).reshape(-1)
    second = cols_second.reshape(-1)
    live_first, live_second = count_first.reshape(-1), count_second.reshape(-1)

    gathered = lax.all_gather(slopes, "out", axis=0, tiled=True)
    partial_first = forward(gathered, None, first, live_first, weight_first, frames, n_in, sub)
    hidden, ordered = hidden_layer(n_out, n_in, partial_first, bias_first)

    partial_second = forward(ordered, sub, second, live_second, weight_second, frames, n_in, sub)
    estimate, rows_second = estimate_layer(n_in, partial_second, bias_second, cotangent)

    spread = adjoint(rows_second, weight_second, second, live_second, n_out)
    rows_first = reduce_layer(n_out, n_in, spread, hidden)
    grad_second = weight_grad(ordered, sub, second, live_second, rows_second, KD2)
    grad_first = weight_grad(gathered, None, first, live_first, rows_first, KD1)
    return (estimate, grad_first, grad_second)


def solution(mesh):
    return jax.shard_map(
        functools.partial(shards, mesh.shape["out"], mesh.shape["in"]),
        mesh=mesh,
        in_specs=(
            P("out", "in"),
            P(None, "in"),
            P("out", "in"),
            P("out", "in", None, None),
            P(("out", "in")),
            P("out", "in"),
            P("out", "in"),
            P("out", "in", None, None),
            P(("out", "in")),
            P(None, ("out", "in")),
        ),
        out_specs=(P(None, ("out", "in")), P("out", "in", None, None), P("out", "in", None, None)),
        check_vma=False,
    )
```

```python
import functools

import jax
import jax.numpy as jnp
from jax import lax
from jax.experimental import pallas as pl
from jax.experimental.pallas import tpu as pltpu
from jax.sharding import PartitionSpec as P

BLK = 256
KD1 = 8
KD2 = 4
VMEM_LIMIT = 48 * 1024 * 1024
F32 = jnp.float32
BF16 = jnp.bfloat16


def params():
    return pltpu.CompilerParams(vmem_limit_bytes=VMEM_LIMIT)


def panel_block(frames, sub):
    return (1, frames, BLK) if sub >= BLK else (BLK // sub, frames, sub)


def panel_place(sub, block):
    if sub >= BLK:
        per = sub // BLK
        return (block // per, 0, block % per)
    return (block, 0, 0)


def read_panel(ref):
    parts = [ref[i] for i in range(ref.shape[0])]
    return parts[0] if len(parts) == 1 else jnp.concatenate(parts, axis=1)


def slot_panel(panels, k):
    if len(panels) > 1:
        return read_panel(panels[k])
    pieces, _, frames, width = panels[0].shape
    return panels[0][:, k].astype(F32).reshape(pieces * frames, width).astype(BF16)


def write_panel(ref, value):
    width = ref.shape[2]
    for i in range(ref.shape[0]):
        ref[i] = value[:, i * width : (i + 1) * width].astype(ref.dtype)


def forward_kernel(slots, cols, counts, *refs):
    panels, weight, out = refs[:-2], refs[-2], refs[-1]
    live = counts[pl.program_id(0)]
    total = None
    for k in range(slots):
        term = jnp.dot(slot_panel(panels, k), weight[0, k], preferred_element_type=F32)
        term = jnp.where(k < live, term, 0.0)
        total = term if total is None else total + term
    write_panel(out, total)


def grad_kernel(slots, cols, counts, *refs):
    panels, delta, out = refs[:-2], refs[-2], refs[-1]
    live = counts[pl.program_id(0)]
    rows = read_panel(delta)
    for k in range(slots):
        term = lax.dot_general(
            slot_panel(panels, k), rows, (((0,), (0,)), ((), ())), preferred_element_type=F32
        )
        out[0, k] = jnp.where(k < live, term, 0.0).astype(out.dtype)


def adjoint_kernel(slots, cols, counts, delta, weight, out, total):
    row = pl.program_id(0)
    live = counts[row]

    @pl.when(row == 0)
    def _():
        total[...] = jnp.zeros_like(total)

    rows = read_panel(delta)
    for k in range(slots):
        term = lax.dot_general(
            rows, weight[0, k], (((1,), (1,)), ((), ())), preferred_element_type=F32
        )
        place = cols[row * slots + k]
        total[place] += jnp.where(k < live, term, 0.0)

    @pl.when(row == pl.num_programs(0) - 1)
    def _():
        pieces, frames, sub = out.shape
        if sub >= BLK:
            per = sub // BLK
            for c in range(total.shape[0]):
                at = (c % per) * BLK
                out[c // per, :, at : at + BLK] = total[c].astype(out.dtype)
        else:
            per = BLK // sub
            for p in range(pieces):
                at = (p % per) * sub
                out[p] = total[p // per, :, at : at + sub].astype(out.dtype)


def panel_specs(slots, frames, sub, inputs):
    if sub is None:
        pieces, _, own, _ = inputs.shape
        return [pl.BlockSpec((pieces, slots, own, BLK), lambda r, cols, counts: (0, r, 0, 0))]

    def spec(k):
        return pl.BlockSpec(
            panel_block(frames, sub),
            lambda r, cols, counts: panel_place(sub, cols[r * slots + k]),
        )

    return [spec(k) for k in range(slots)]


def row_spec(frames, sub):
    return pl.BlockSpec(panel_block(frames, sub), lambda r, cols, counts: panel_place(sub, r))


def weight_spec(slots):
    return pl.BlockSpec((1, slots, BLK, BLK), lambda r, cols, counts: (r, 0, 0, 0))


def forward(inputs, in_sub, cols, counts, weight, frames, pieces, sub):
    rows, slots = weight.shape[:2]
    return pl.pallas_call(
        functools.partial(forward_kernel, slots),
        grid_spec=pltpu.PrefetchScalarGridSpec(
            num_scalar_prefetch=2,
            grid=(rows,),
            in_specs=panel_specs(slots, frames, in_sub, inputs) + [weight_spec(slots)],
            out_specs=row_spec(frames, sub),
        ),
        out_shape=jax.ShapeDtypeStruct((pieces, frames, sub), F32),
        compiler_params=params(),
    )(cols, counts, *([inputs] * (1 if in_sub is None else slots)), weight)


def weight_grad(inputs, in_sub, cols, counts, delta, slots):
    pieces, frames, sub = delta.shape
    rows = pieces * sub // BLK
    return pl.pallas_call(
        functools.partial(grad_kernel, slots),
        grid_spec=pltpu.PrefetchScalarGridSpec(
            num_scalar_prefetch=2,
            grid=(rows,),
            in_specs=panel_specs(slots, frames, in_sub, inputs) + [row_spec(frames, sub)],
            out_specs=weight_spec(slots),
        ),
        out_shape=jax.ShapeDtypeStruct((rows, slots, BLK, BLK), BF16),
        cost_estimate=pl.CostEstimate(
            flops=2 * rows * slots * frames * BLK * BLK,
            bytes_accessed=2 * rows * slots * BLK * (BLK + frames),
            transcendentals=0,
        ),
        compiler_params=params(),
    )(cols, counts, *([inputs] * (1 if in_sub is None else slots)), delta)


def adjoint(delta, weight, cols, counts, out_pieces):
    pieces, frames, sub = delta.shape
    rows, slots = weight.shape[:2]
    return pl.pallas_call(
        functools.partial(adjoint_kernel, slots),
        grid_spec=pltpu.PrefetchScalarGridSpec(
            num_scalar_prefetch=2,
            grid=(rows,),
            in_specs=[row_spec(frames, sub), weight_spec(slots)],
            out_specs=pl.BlockSpec((out_pieces, frames, sub), lambda r, cols, counts: (0, 0, 0)),
            scratch_shapes=[pltpu.VMEM((out_pieces * sub // BLK, frames, BLK), F32)],
        ),
        out_shape=jax.ShapeDtypeStruct((out_pieces, frames, sub), BF16),
        compiler_params=params(),
    )(cols, counts, delta, weight)


MESH = pl.DeviceIdType.MESH
STEP = 16
SIDE = 4


def by_rows(frames, body):
    def turn(i, carry):
        body(pl.ds(pl.multiple_of(i * STEP, STEP), STEP))
        return carry

    lax.fori_loop(0, frames // STEP, turn, 0)


def remote(source, target, send, recv, peer):
    return pltpu.make_async_remote_copy(
        src_ref=source,
        dst_ref=target,
        send_sem=send,
        recv_sem=recv,
        device_id=peer,
        device_id_type=MESH,
    )


def greet(peers):
    barrier = pltpu.get_barrier_semaphore()
    for peer in peers:
        pl.semaphore_signal(barrier, inc=1, device_id=peer, device_id_type=MESH)
    pl.semaphore_wait(barrier, len(peers))


def in_peers(n_in):
    me = lax.axis_index("in")
    return [{"in": lax.rem(me + t, n_in)} for t in range(1, n_in)]


def out_place(n_out):
    me = lax.axis_index("out")
    inner = lax.rem(me, SIDE)
    core = lax.rem(me, 2)
    column = lax.rem(lax.div(me, 2), 2)
    return me, lax.div(me, SIDE), inner, me + 1 - 2 * core, me + 2 - 4 * column


def out_peers(n_out):
    me, outer, inner, core_peer, x_peer = out_place(n_out)
    count = n_out // SIDE
    far = [{"out": lax.rem(outer + t, count) * SIDE + inner} for t in range(1, count)]
    return [{"out": core_peer}, {"out": x_peer}] + far


def exchange_start(n_in, partial, leaving, arriving, send, recv):
    copies = []
    for t, peer in enumerate(in_peers(n_in)):
        def cast(at, t=t, peer=peer):
            leaving[t, at, :] = partial[peer["in"], at, :].astype(BF16)

        by_rows(partial.shape[1], cast)
        copy = remote(leaving.at[t], arriving.at[t], send.at[t], recv.at[t], peer)
        copy.start()
        copies.append(copy)
    for copy in copies:
        copy.wait()


def exchanged(n_in, partial, arriving, bias, at):
    total = partial[lax.axis_index("in"), at, :]
    for t in range(n_in - 1):
        total = total + arriving[t, at, :].astype(F32)
    return total + bias[...]


def share_in(n_in, rows, send, recv):
    me = lax.axis_index("in")
    copies = []
    for t, peer in enumerate(in_peers(n_in)):
        copy = remote(rows.at[me], rows.at[me], send.at[t], recv.at[t], peer)
        copy.start()
        copies.append(copy)
    for copy in copies:
        copy.wait()


def gather_out(n_out, hidden, ordered, send, recv, own):
    me, outer, inner, core_peer, x_peer = out_place(n_out)
    count = n_out // SIDE
    copies = []

    def forward_to(source, block, target):
        k = len(copies)
        copy = remote(source, ordered.at[block], send.at[k], recv.at[block], {"out": target})
        copy.start()
        copies.append(copy)

    def arrived(block):
        remote(hidden, ordered.at[block], send.at[0], recv.at[block], {"out": core_peer}).wait_recv()

    def held(t, place):
        return lax.rem(outer + t, count) * SIDE + place

    for t in range(1, count):
        forward_to(hidden, me, held(t, inner))
    forward_to(hidden, me, x_peer)
    forward_to(hidden, me, core_peer)
    keep = pltpu.make_async_copy(hidden, ordered.at[me], own)
    keep.start()
    across = lax.rem(x_peer, SIDE)
    for t in range(1, count + 1):
        if t < count:
            block = held(t, inner)
            arrived(block)
            forward_to(ordered.at[block], block, x_peer)
            forward_to(ordered.at[block], block, core_peer)
        block = held(t - 1, across)
        arrived(block)
        forward_to(ordered.at[block], block, core_peer)
    for t in range(count):
        for place in (lax.rem(core_peer, SIDE), SIDE - 1 - inner):
            arrived(held(t, place))
    for copy in copies:
        copy.wait_send()
    keep.wait()


def hidden_kernel(
    n_out, n_in, partial, bias, hidden, ordered, leaving, arriving, in_send, in_recv, send, recv, own
):
    frames = hidden.shape[0]
    greet(in_peers(n_in) + out_peers(n_out))
    exchange_start(n_in, partial, leaving, arriving, in_send, in_recv)

    def finish(at):
        hidden[at, :] = jnp.tanh(exchanged(n_in, partial, arriving, bias, at)).astype(BF16)

    by_rows(frames, finish)
    gather_out(n_out, hidden, ordered, send, recv, own)


def estimate_kernel(
    n_in, partial, bias, cotangent, estimate, rows, leaving, arriving, in_send, in_recv, send, recv
):
    greet(in_peers(n_in))
    exchange_start(n_in, partial, leaving, arriving, in_send, in_recv)
    me = lax.axis_index("in")

    def finish(at):
        value = jnp.tanh(exchanged(n_in, partial, arriving, bias, at)).astype(BF16)
        estimate[at, :] = value
        wide = value.astype(F32)
        rows[me, at, :] = (cotangent[at, :].astype(F32) * (1.0 - wide * wide)).astype(BF16)

    by_rows(estimate.shape[0], finish)
    share_in(n_in, rows, send, recv)


def reduce_kernel(
    n_out, n_in, spread, hidden, rows,
    from_core, to_x, from_x, to_z, from_z,
    core_send, core_recv, x_send, x_recv, z_send, z_recv, in_send, in_recv,
):
    frames = hidden.shape[0]
    count = n_out // SIDE
    greet(in_peers(n_in) + out_peers(n_out))
    me, outer, inner, core_peer, x_peer = out_place(n_out)
    across = lax.rem(x_peer, SIDE)
    core_inner, core_across = lax.rem(core_peer, SIDE), SIDE - 1 - inner

    def held(t, place):
        return lax.rem(outer + t, count) * SIDE + place

    core_copies, x_copies, z_copies = [], [], []
    for t in range(1, count + 1):
        for place in (core_across, core_inner):
            k = len(core_copies)
            copy = remote(
                spread.at[held(t, place)], from_core.at[k], core_send.at[k], core_recv.at[k],
                {"out": core_peer},
            )
            copy.start()
            core_copies.append(copy)

    def column_sum(t, at):
        total = spread[held(t, inner), at, :].astype(F32)
        total = total + from_core[2 * t - 1, at, :].astype(F32)
        return total + from_x[t - 1, at, :].astype(F32)

    for t in range(1, count + 2):
        if t <= count:
            core_copies[2 * t - 2].wait_recv()

            def add_core(at, t=t):
                total = spread[held(t, across), at, :].astype(F32)
                to_x[t - 1, at, :] = (total + from_core[2 * t - 2, at, :].astype(F32)).astype(BF16)

            by_rows(frames, add_core)
            copy = remote(
                to_x.at[t - 1], from_x.at[t - 1], x_send.at[t - 1], x_recv.at[t - 1],
                {"out": x_peer},
            )
            copy.start()
            x_copies.append(copy)
        s = t - 1
        if s >= 1:
            core_copies[2 * s - 1].wait_recv()
            x_copies[s - 1].wait_recv()
        if 1 <= s < count:

            def add_x(at, s=s):
                to_z[s - 1, at, :] = column_sum(s, at).astype(BF16)

            by_rows(frames, add_x)
            copy = remote(
                to_z.at[s - 1], from_z.at[s - 1], z_send.at[s - 1], z_recv.at[s - 1],
                {"out": held(s, inner)},
            )
            copy.start()
            z_copies.append(copy)
    for copy in z_copies:
        copy.wait_recv()
    place = lax.axis_index("in")

    def finish(at):
        total = column_sum(count, at)
        for s in range(count - 1):
            total = total + from_z[s, at, :].astype(F32)
        wide = hidden[at, :].astype(F32)
        rows[place, at, :] = (total * (1.0 - wide * wide)).astype(BF16)

    by_rows(frames, finish)
    share_in(n_in, rows, in_send, in_recv)
    for copy in core_copies + x_copies + z_copies:
        copy.wait_send()


def whole_specs(count):
    return [pl.BlockSpec(memory_space=pltpu.VMEM)] * count


def dma(count):
    return pltpu.SemaphoreType.DMA((count,))


def remote_params(collective_id):
    return pltpu.CompilerParams(
        collective_id=collective_id, has_side_effects=True, vmem_limit_bytes=VMEM_LIMIT
    )


def hidden_layer(n_out, n_in, partial, bias):
    _, frames, sub = partial.shape
    return pl.pallas_call(
        functools.partial(hidden_kernel, n_out, n_in),
        out_shape=(
            jax.ShapeDtypeStruct((frames, sub), BF16),
            jax.ShapeDtypeStruct((n_out, frames, sub), BF16),
        ),
        in_specs=whole_specs(2),
        out_specs=(pl.BlockSpec(memory_space=pltpu.VMEM), pl.BlockSpec(memory_space=pl.ANY)),
        scratch_shapes=[
            pltpu.VMEM((n_in - 1, frames, sub), BF16),
            pltpu.VMEM((n_in - 1, frames, sub), BF16),
            dma(n_in - 1),
            dma(n_in - 1),
            dma(n_out),
            dma(n_out),
            pltpu.SemaphoreType.DMA,
        ],
        compiler_params=remote_params(1),
    )(partial, bias.reshape(1, -1))


def estimate_layer(n_in, partial, bias, cotangent):
    _, frames, sub = partial.shape
    return pl.pallas_call(
        functools.partial(estimate_kernel, n_in),
        out_shape=(
            jax.ShapeDtypeStruct((frames, sub), BF16),
            jax.ShapeDtypeStruct((n_in, frames, sub), BF16),
        ),
        in_specs=whole_specs(3),
        out_specs=tuple(whole_specs(2)),
        scratch_shapes=[
            pltpu.VMEM((n_in - 1, frames, sub), BF16),
            pltpu.VMEM((n_in - 1, frames, sub), BF16),
            dma(n_in - 1),
            dma(n_in - 1),
            dma(n_in - 1),
            dma(n_in - 1),
        ],
        compiler_params=remote_params(2),
    )(partial, bias.reshape(1, -1), cotangent)


def reduce_layer(n_out, n_in, spread, hidden):
    _, frames, sub = spread.shape
    count = n_out // SIDE
    blocks = lambda n: pltpu.VMEM((n, frames, sub), BF16)
    return pl.pallas_call(
        functools.partial(reduce_kernel, n_out, n_in),
        out_shape=jax.ShapeDtypeStruct((n_in, frames, sub), BF16),
        in_specs=whole_specs(2),
        out_specs=pl.BlockSpec(memory_space=pltpu.VMEM),
        scratch_shapes=[
            blocks(2 * count), blocks(count), blocks(count), blocks(count - 1), blocks(count - 1),
            dma(2 * count), dma(2 * count), dma(count), dma(count), dma(count - 1), dma(count - 1),
            dma(n_in - 1), dma(n_in - 1),
        ],
        compiler_params=remote_params(3),
    )(spread, hidden)


def slopes_kernel(n_out, cols, slopes, panels, packed, send, recv, own):
    slots = packed.shape[1]
    me, outer, inner, _, _ = out_place(n_out)
    count = n_out // SIDE
    greet([{"out": lax.rem(me + t, n_out)} for t in range(1, n_out)])

    def pack(target):
        def turn(i, carry):
            for j in range(8):
                at = i * 8 + j
                packed[target, at] = slopes[cols[target * slots + at]]
            return carry

        lax.fori_loop(0, slots // 8, turn, 0)

    copies = []
    order = sorted(range(count), key=lambda t: -min(t, count - t))
    for t in order:
        for step in range(SIDE):
            k = t * SIDE + step
            if k == 0:
                continue
            target = lax.rem(outer + t, count) * SIDE + lax.rem(inner + step, SIDE)
            pack(target)
            copy = remote(
                packed.at[target], panels.at[me], send.at[k], recv.at[k], {"out": target}
            )
            copy.start()
            copies.append(copy)
    pack(me)
    keep = pltpu.make_async_copy(packed.at[me], panels.at[me], own)
    keep.start()
    for copy in copies:
        copy.wait()
    keep.wait()


def slope_panels(n_out, slopes, cols):
    frames = slopes.shape[0]
    slots = cols.shape[0] // n_out
    shape = (n_out, slots, frames, BLK)
    return pl.pallas_call(
        functools.partial(slopes_kernel, n_out),
        out_shape=jax.ShapeDtypeStruct(shape, BF16),
        in_specs=[pl.BlockSpec(memory_space=pltpu.SMEM), pl.BlockSpec(memory_space=pltpu.VMEM)],
        out_specs=pl.BlockSpec(memory_space=pl.ANY),
        scratch_shapes=[
            pltpu.VMEM(shape, BF16), dma(n_out), dma(n_out), pltpu.SemaphoreType.DMA
        ],
        compiler_params=remote_params(4),
    )(cols, slopes.reshape(frames, -1, BLK).transpose(1, 0, 2))


def first_kernel(
    n_out, n_in, cols, counts, slopes, weight_hbm, bias, hidden, ordered, kept,
    packed, panels, weight, leaving, arriving, mine,
    p_send, p_recv, w_sem, kept_sem, in_send, in_recv, send, recv, own,
):
    frames = hidden.shape[0]
    rows, depth = weight.shape[:2]
    chunk = panels.shape[2]
    slots, per = chunk * n_in, chunk // depth
    me, outer, inner, _, _ = out_place(n_out)
    place = lax.axis_index("in")
    count = n_out // SIDE
    greet(in_peers(n_in) + [{"out": lax.rem(me + t, n_out)} for t in range(1, n_out)])
    load = pltpu.make_async_copy(weight_hbm, weight, w_sem)
    load.start()

    def pack(into, h, target, at, piece):
        def turn(i, carry):
            for j in range(8):
                k = i * 8 + j
                into[h, at, k] = slopes[cols[target * slots + piece * chunk + k]]
            return carry

        lax.fori_loop(0, chunk // 8, turn, 0)

    order = sorted(range(count), key=lambda t: -min(t, count - t))
    copies = []
    for h in range(n_in):
        piece = lax.rem(place + 1 + h, n_in)
        sent = []
        for t in order:
            for step in range(SIDE):
                k = t * SIDE + step
                if k == 0:
                    continue
                target = lax.rem(outer + t, count) * SIDE + lax.rem(inner + step, SIDE)
                pack(packed, h, target, target, piece)
                copy = remote(
                    packed.at[h, target], panels.at[h, me], p_send.at[h, k], p_recv.at[h, k],
                    {"out": target},
                )
                copy.start()
                sent.append(copy)
        pack(panels, h, me, me, piece)
        copies.append(sent)

    load.wait()
    saves, exchanges = [], []
    for h, peer in enumerate(in_peers(n_in) + [None]):
        piece = lax.rem(place + 1 + h, n_in)
        for copy in copies[h]:
            copy.wait_recv()
        save = pltpu.make_async_copy(
            panels.at[h], kept.at[:, pl.ds(piece * chunk, chunk)], kept_sem.at[h]
        )
        save.start()
        saves.append(save)
        for j in range(per):
            row = piece * per + j
            live = counts[row]
            total = None
            for k in range(depth):
                panel = panels[h, :, j * depth + k].astype(F32).reshape(frames, BLK).astype(BF16)
                term = jnp.dot(panel, weight[row, k], preferred_element_type=F32)
                term = jnp.where(k < live, term, 0.0)
                total = term if total is None else total + term
            if peer is None:
                mine[:, j * BLK : (j + 1) * BLK] = total
            else:
                leaving[h, :, j * BLK : (j + 1) * BLK] = total.astype(BF16)
        if peer is not None:
            copy = remote(leaving.at[h], arriving.at[h], in_send.at[h], in_recv.at[h], peer)
            copy.start()
            exchanges.append(copy)
    for copy in exchanges:
        copy.wait_recv()

    def finish(at):
        total = mine[at, :]
        for t in range(n_in - 1):
            total = total + arriving[t, at, :].astype(F32)
        hidden[at, :] = jnp.tanh(total + bias[...]).astype(BF16)

    by_rows(frames, finish)
    gather_out(n_out, hidden, ordered, send, recv, own)
    for copy in sum(copies, []) + exchanges:
        copy.wait_send()
    for save in saves:
        save.wait()


def first_layer(n_out, n_in, slopes, cols, counts, weight, bias):
    own_frames = slopes.shape[0]
    frames, sub = own_frames * n_out, bias.shape[0]
    slots = cols.shape[0] // n_out
    split = (n_in, n_out, slots // n_in, own_frames, BLK)
    smem = pl.BlockSpec(memory_space=pltpu.SMEM)
    vmem = pl.BlockSpec(memory_space=pltpu.VMEM)
    anywhere = pl.BlockSpec(memory_space=pl.ANY)
    return pl.pallas_call(
        functools.partial(first_kernel, n_out, n_in),
        out_shape=(
            jax.ShapeDtypeStruct((frames, sub), BF16),
            jax.ShapeDtypeStruct((n_out, frames, sub), BF16),
            jax.ShapeDtypeStruct((n_out, slots, own_frames, BLK), BF16),
        ),
        in_specs=[smem, smem, vmem, anywhere, vmem],
        out_specs=(vmem, anywhere, anywhere),
        scratch_shapes=[
            pltpu.VMEM(split, BF16),
            pltpu.VMEM(split, BF16),
            pltpu.VMEM(weight.shape, BF16),
            pltpu.VMEM((n_in - 1, frames, sub), BF16),
            pltpu.VMEM((n_in - 1, frames, sub), BF16),
            pltpu.VMEM((frames, sub), F32),
            pltpu.SemaphoreType.DMA((n_in, n_out)),
            pltpu.SemaphoreType.DMA((n_in, n_out)),
            pltpu.SemaphoreType.DMA,
            dma(n_in), dma(n_in - 1), dma(n_in - 1), dma(n_out), dma(n_out),
            pltpu.SemaphoreType.DMA,
        ],
        compiler_params=remote_params(5),
    )(
        cols, counts, slopes.reshape(own_frames, -1, BLK).transpose(1, 0, 2), weight,
        bias.reshape(1, -1),
    )


def shards(
    n_out,
    n_in,
    slopes,
    cols_first,
    count_first,
    weight_first,
    bias_first,
    cols_second,
    count_second,
    weight_second,
    bias_second,
    cotangent,
):
    rows = weight_first.shape[0]
    frames = slopes.shape[0] * n_out
    sub = bias_first.shape[0]
    second = cols_second.reshape(-1)
    live_first, live_second = count_first.reshape(-1), count_second.reshape(-1)

    all_cols = cols_first.reshape(-1)
    if sub >= BLK:
        hidden, ordered, panels = first_layer(
            n_out, n_in, slopes, all_cols, live_first, weight_first, bias_first
        )
    else:
        panels = slope_panels(n_out, slopes, all_cols)
        partial_first = forward(panels, None, second, live_first, weight_first, frames, n_in, sub)
        hidden, ordered = hidden_layer(n_out, n_in, partial_first, bias_first)

    partial_second = forward(ordered, sub, second, live_second, weight_second, frames, n_in, sub)
    estimate, rows_second = estimate_layer(n_in, partial_second, bias_second, cotangent)

    spread = adjoint(rows_second, weight_second, second, live_second, n_out)
    rows_first = reduce_layer(n_out, n_in, spread, hidden)
    grad_second = weight_grad(ordered, sub, second, live_second, rows_second, KD2)
    grad_first = weight_grad(panels, None, second, live_first, rows_first, KD1)
    return (estimate, grad_first, grad_second)


def solution(mesh):
    return jax.shard_map(
        functools.partial(shards, mesh.shape["out"], mesh.shape["in"]),
        mesh=mesh,
        in_specs=(
            P("out", "in"),
            P(None, "in"),
            P("out", "in"),
            P("out", "in", None, None),
            P(("out", "in")),
            P("out", "in"),
            P("out", "in"),
            P("out", "in", None, None),
            P(("out", "in")),
            P(None, ("out", "in")),
        ),
        out_specs=(P(None, ("out", "in")), P("out", "in", None, None), P("out", "in", None, None)),
        check_vma=False,
    )
```
